32 devices in a mesh: wide: 16 (over z, y, x), narrow: 2 (over core).
Axes of the slice: x: 2, y: 2, z: 4, core: 2. Of those that a mesh axis runs over, the one named last changes fastest.
Arguments:
- panel: float32 [8, 1048576], P(None, ('wide', 'narrow')), may hold values from -0.25 to 0.25
- signs: int32 [1048576], P(('wide', 'narrow')), may hold values from -1 to 1, as said below
- samples: int32 [4096], P(('wide', 'narrow')), may hold values from 0 to 1048575, as said below
Outputs:
- sketch: float32 [8, 4096], P(None, ('wide', 'narrow'))
The draws below stay inside these ranges and needn't reach their ends.
Inputs may be any that keep to these rules, and one draw needn't show every extreme that they name: `signs`: every entry is +1 or -1. `samples`: for every k, entries 128 * k to 128 * (k + 1) - 1 are distinct, increasing, and lie among rows 32768 * k to 32768 * (k + 1) - 1.
All inputs are finite; a program needn't handle non-finite values.
Results may differ from the reference program's by a relative error of at most 0.000071.
Values sent between devices are 32-bit elements; how exact they have to be, the bound alone decides.
No kernel may reach another device: no remote copies, remote signals or barrier semaphores. Data moves between devices by JAX's collectives and lax.ppermute only.
A program may use at most 64 MiB of HBM per device.

```python
import math
import jax
import jax.numpy as jnp

COLS = 8
ROWS_DEV = 32768
SAMP_DEV = 128
ROWS = 1048576
SAMPLES = 4096


def draw_signs(key, part):
    flips = jax.random.randint(key, (ROWS,), 0, 2)
    return (2 * flips - 1).astype(jnp.int32)


def draw_samples(key, part):
    blocks = SAMPLES // SAMP_DEV
    keys = jax.random.split(jax.random.fold_in(key, 7), blocks)

    def one_block(block_key):
        order = jax.random.permutation(block_key, ROWS_DEV)[:SAMP_DEV]
        return jnp.sort(order)
    chosen = jax.vmap(one_block)(keys)
    chosen = chosen.at[0, 0].set(0)
    chosen = chosen.at[blocks - 1, SAMP_DEV - 1].set(ROWS_DEV - 1)
    starts = (jnp.arange(blocks) * ROWS_DEV)[:, None]
    return (chosen + starts).reshape(SAMPLES).astype(jnp.int32)


def level_of(own_key, dims, pieces, smallest, largest):
    factor_of = 1.0
    for dim, shards_of in pieces:
        draws = jax.random.uniform(jax.random.fold_in(jax.random.fold_in(own_key, 6), dim), (shards_of,), jnp.float32, smallest / len(pieces), largest / len(pieces))
        factor_of = factor_of * jnp.repeat(jnp.exp(draws), dims[dim] // shards_of).reshape((-1,) + (1,) * (len(dims) - 1 - dim))
    return factor_of


def noise(key, extent, deviation, reach, cuts=(), held_as=jnp.bfloat16):
    entries = jax.random.normal(key, extent, jnp.float32) * deviation
    if len(cuts) > 0:
        entries = level_of(key, extent, cuts, -0.22, 0.18) * entries
    return jnp.clip(entries, min=-reach, max=reach).astype(held_as)


def setup_inputs(seed: int = 0) -> dict:
    streams_of = jax.random.split(jax.random.key(seed), 4)
    panel = noise(streams_of[0], (COLS, ROWS), 0.03125, 0.25, ((1, 32),), jnp.float32)
    signs = draw_signs(jax.random.fold_in(streams_of[3], 71), 0)
    samples = draw_samples(jax.random.fold_in(streams_of[3], 71), 0)
    return {"panel": panel, "signs": signs, "samples": samples}


def reference(panel, signs, samples):
    values = panel * signs.astype(jnp.float32)[None, :]
    total = values.shape[1]
    levels = total.bit_length() - 1
    for level in range(levels):
        half = 2 ** level
        shaped = values.reshape(COLS, total // (2 * half), 2, half)
        first = shaped[:, :, 0, :]
        second = shaped[:, :, 1, :]
        values = jnp.stack([first + second, first - second], axis=2).reshape(COLS, total)
    scale = 1.0 / math.sqrt(SAMPLES)
    return jnp.take(values, samples, axis=1) * jnp.float32(scale)
```

```python
import functools
import math

import jax
import jax.numpy as jnp
from jax import lax
from jax.experimental import pallas as pl
from jax.experimental.pallas import tpu as pltpu
from jax.sharding import PartitionSpec as P

LANES = 128
LOW = 256
AXES = ("wide", "narrow")
VMEM_LIMIT = 40 << 20


def vmem():
    return pl.BlockSpec(memory_space=pltpu.VMEM)


def parity(value):
    return bin(value).count("1") & 1


def hadamard_rows(order):
    row = lax.broadcasted_iota(jnp.int32, (order, order), 0)
    col = lax.broadcasted_iota(jnp.int32, (order, order), 1)
    bits = row & col
    shift = order.bit_length() // 2
    while shift:
        bits = bits ^ (bits >> shift)
        shift //= 2
    sign = (1 - 2 * (bits & 1)).astype(jnp.float32).astype(jnp.bfloat16)
    return jnp.concatenate([sign, sign], axis=0)


def two_parts(values):
    high = values.astype(jnp.bfloat16)
    low = (values - high.astype(jnp.float32)).astype(jnp.bfloat16)
    return jnp.concatenate([high, low], axis=1)


def butterfly(values):
    values = list(values)
    step = 1
    while step < len(values):
        for at in range(len(values)):
            if not at & step:
                first, second = values[at], values[at | step]
                values[at], values[at | step] = first + second, first - second
        step *= 2
    return values


def transform_kernel(outer, inner, mine_ref, other_ref, mine_signs_ref, other_signs_ref, even_ref, odd_ref, even_mid, odd_mid):
    core = lax.axis_index("narrow") & 1
    flip = (1 - 2 * core).astype(jnp.float32)
    cols = mine_ref.shape[0]
    tiles = LOW // LANES

    def load(group, tile):
        at = group * tiles + tile
        lanes = pl.ds(pl.multiple_of(at * LANES, LANES), LANES)
        mine_sign = mine_signs_ref[pl.ds(at, 1), :].astype(jnp.float32)
        other_sign = other_signs_ref[pl.ds(at, 1), :].astype(jnp.float32)
        mine = mine_ref[:, lanes] * mine_sign
        other = other_ref[:, lanes] * other_sign
        return other + flip * mine, mine - flip * other

    def first_pass(b, carry):
        for tile in range(tiles):
            pairs = [load(a * inner + b, tile) for a in range(outer)]
            for mid, values in ((even_mid, [p[0] for p in pairs]), (odd_mid, [p[1] for p in pairs])):
                for a, value in enumerate(butterfly(values)):
                    rows = pl.ds(pl.multiple_of((a * inner + b) * cols, cols), cols)
                    mid[rows, tile * LANES : (tile + 1) * LANES] = value
        return carry

    lax.fori_loop(0, inner, first_pass, 0)
    matrix = hadamard_rows(LOW)

    def second_pass(a, carry):
        rows = pl.ds(pl.multiple_of(a * inner * cols, inner * cols), inner * cols)
        for mid, out_ref in ((even_mid, even_ref), (odd_mid, odd_ref)):
            block = mid[rows, :]
            values = butterfly([block[b * cols : (b + 1) * cols] for b in range(inner)])
            block = two_parts(jnp.concatenate(values, axis=0))
            block = jnp.dot(block, matrix, preferred_element_type=jnp.float32)
            out_ref[rows, :] = two_parts(block)
        return carry

    lax.fori_loop(0, outer, second_pass, 0)


def transform(mine, other, mine_signs, other_signs):
    cols, rows = mine.shape
    groups = rows // LOW
    outer = 1 << (groups.bit_length() - 1) // 2
    inner = groups // outer
    shape = (groups * cols, 2 * LOW)
    return pl.pallas_call(
        functools.partial(transform_kernel, outer, inner),
        out_shape=[jax.ShapeDtypeStruct(shape, jnp.bfloat16)] * 2,
        in_specs=[vmem()] * 4,
        out_specs=[vmem()] * 2,
        scratch_shapes=[pltpu.VMEM((groups * cols, LOW), jnp.float32)] * 2,
        compiler_params=pltpu.CompilerParams(vmem_limit_bytes=VMEM_LIMIT),
        cost_estimate=pl.CostEstimate(flops=8 * cols * rows * LOW, bytes_accessed=20 * cols * rows, transcendentals=0),
        name="transform",
    )(mine, other, mine_signs.reshape(rows // LANES, LANES), other_signs.reshape(rows // LANES, LANES))


def gather_kernel(first, groups, cols, even_ref, odd_ref, offsets_ref, out_ref):
    count = offsets_ref.shape[0]
    offsets = offsets_ref[...]
    samp = offsets.shape[1]
    by_parity = [[t for t in range(count) if parity(first + t) == p] for p in range(2)]
    for table_ref, targets in zip((even_ref, odd_ref), by_parity):
        for at in range(0, len(targets), 2):
            pair = targets[at : at + 2]
            offset = jnp.concatenate([offsets[t : t + 1] for t in pair], axis=1)
            width = offset.shape[1]
            low = offset & (LOW - 1)
            high = jnp.broadcast_to(offset // LOW & (groups - 1), (cols, width))
            rows = lax.broadcasted_iota(jnp.int32, (LOW, width), 0)
            chosen = (rows == low).astype(jnp.float32).astype(jnp.bfloat16)
            chosen = jnp.concatenate([chosen, chosen], axis=0)
            picked = jnp.dot(table_ref[...], chosen, preferred_element_type=jnp.float32)
            sums = [jnp.zeros((cols, width), jnp.float32) for _ in range(2)]
            for g in range(groups):
                block = picked[g * cols : (g + 1) * cols]
                sums[g % 2] = jnp.where(high == g, block, sums[g % 2])
            total = sums[0] + sums[1]
            for i, t in enumerate(pair):
                out_ref[t] = total[:, i * samp : (i + 1) * samp]


def gather(first, cols, groups, even, odd, offsets):
    count, samp = offsets.shape
    return pl.pallas_call(
        functools.partial(gather_kernel, first, groups, cols),
        out_shape=jax.ShapeDtypeStruct((count, cols, samp), jnp.float32),
        in_specs=[vmem()] * 3,
        out_specs=vmem(),
        compiler_params=pltpu.CompilerParams(vmem_limit_bytes=VMEM_LIMIT),
        cost_estimate=pl.CostEstimate(
            flops=4 * groups * cols * LOW * count * samp, bytes_accessed=4 * groups * cols * LOW, transcendentals=0
        ),
        name="gather",
    )(even, odd, offsets)


def per_device(panel, signs, samples):
    cols, rows = panel.shape
    samp = samples.shape[0]
    n_wide = lax.axis_size("wide")
    n_narrow = lax.axis_size("narrow")
    wide_bits = n_wide.bit_length() - 1
    narrow_bits = n_narrow.bit_length() - 1
    n_all = n_wide * n_narrow
    wide_me = lax.axis_index("wide")
    narrow_me = lax.axis_index("narrow")

    def across(values, mask):
        return lax.ppermute(values, AXES, [(i, i ^ mask) for i in range(n_all)])

    asked = samples
    for bit in range(wide_bits):
        asked = jnp.concatenate([asked, across(asked, n_narrow << bit | 1)])
    asked = asked.reshape(n_wide, samp)

    for bit in range(1, narrow_bits):
        if bit == 1:
            panel = panel * signs.astype(jnp.float32)[None, :]
            signs = jnp.ones_like(signs)
        upper = narrow_me >> bit & 1 == 1
        partner = across(panel, 1 << bit)
        panel = jnp.where(upper, partner - panel, panel + partner)
    even, odd = transform(panel, across(panel, 1), signs, across(signs, 1))

    groups = rows // LOW
    half = n_wide // 2
    near = gather(0, cols, groups, even, odd, asked[:half])
    far = gather(half, cols, groups, even, odd, asked[half:])
    for bit in reversed(range(wide_bits)):
        sign = (1 - 2 * (wide_me >> bit & 1)).astype(jnp.float32)
        total = across(far, n_narrow << bit | 1) + sign * near
        near, far = total[: 1 << bit >> 1], total[1 << bit >> 1 :]
    return total[0] * jnp.float32(1.0 / math.sqrt(samp * n_all))


def solution(mesh):
    in_specs = (P(None, AXES), P(AXES), P(AXES))
    return jax.shard_map(per_device, mesh=mesh, in_specs=in_specs, out_specs=P(None, AXES), check_vma=False)
```

```python
import functools
import math

import jax
import jax.numpy as jnp
from jax import lax
from jax.experimental import pallas as pl
from jax.experimental.pallas import tpu as pltpu
from jax.sharding import PartitionSpec as P

LANES = 128
LOW = 256
AXES = ("wide", "narrow")
VMEM_LIMIT = 40 << 20


def vmem():
    return pl.BlockSpec(memory_space=pltpu.VMEM)


def parity(value):
    return bin(value).count("1") & 1


def hadamard_rows(order):
    row = lax.broadcasted_iota(jnp.int32, (order, order), 0)
    col = lax.broadcasted_iota(jnp.int32, (order, order), 1)
    bits = row & col
    shift = order.bit_length() // 2
    while shift:
        bits = bits ^ (bits >> shift)
        shift //= 2
    sign = (1 - 2 * (bits & 1)).astype(jnp.float32).astype(jnp.bfloat16)
    return jnp.concatenate([sign, sign], axis=0)


def two_parts(values):
    high = values.astype(jnp.bfloat16)
    low = (values - high.astype(jnp.float32)).astype(jnp.bfloat16)
    return jnp.concatenate([high, low], axis=1)


def butterfly(values):
    values = list(values)
    step = 1
    while step < len(values):
        for at in range(len(values)):
            if not at & step:
                first, second = values[at], values[at | step]
                values[at], values[at | step] = first + second, first - second
        step *= 2
    return values


def first_pass(outer, inner, values_ref, signs_ref, mid, a):
    cols = values_ref.shape[0]
    tiles = LOW // LANES
    for tile in range(tiles):
        values = []
        for b in range(inner):
            at = (a * inner + b) * tiles + tile
            lanes = pl.ds(pl.multiple_of(at * LANES, LANES), LANES)
            values.append(values_ref[:, lanes] * signs_ref[pl.ds(at, 1), :].astype(jnp.float32))
        for b, value in enumerate(butterfly(values)):
            rows = pl.ds(pl.multiple_of((a * inner + b) * cols, cols), cols)
            mid[rows, tile * LANES : (tile + 1) * LANES] = value


def second_pass(outer, inner, cols, mid, parts):
    def step(b, carry):
        values = [mid[pl.ds(pl.multiple_of((a * inner + b) * cols, cols), cols), :] for a in range(outer)]
        block = two_parts(jnp.concatenate(butterfly(values), axis=0))
        parts[pl.ds(pl.multiple_of(b * outer * cols, outer * cols), outer * cols), :] = block
        return carry

    lax.fori_loop(0, inner, step, 0)


def own_kernel(outer, inner, values_hbm, signs_hbm, samples_ref, out_ref, list_ref, values_ref, signs_ref, mid, parts, sems):
    cols, rows = values_hbm.shape
    block = rows // outer
    signs_copy = pltpu.make_async_copy(signs_hbm, signs_ref, sems.at[outer])
    copies = [
        pltpu.make_async_copy(
            values_hbm.at[:, pl.ds(a * block, block)], values_ref.at[:, pl.ds(a * block, block)], sems.at[a]
        )
        for a in range(outer)
    ]
    signs_copy.start()
    for copy in copies:
        copy.start()
    list_ref[...] = samples_ref[...]
    matrix = hadamard_rows(LOW)
    signs_copy.wait()
    for a, copy in enumerate(copies):
        copy.wait()
        first_pass(outer, inner, values_ref, signs_ref, mid, a)
    second_pass(outer, inner, cols, mid, parts)
    out_ref[...] = jnp.dot(parts[...], matrix, preferred_element_type=jnp.float32)


def other_kernel(outer, inner, values_ref, signs_ref, mine_ref, even_ref, odd_ref, mid, parts):
    cols = values_ref.shape[0]

    def step(a, carry):
        first_pass(outer, inner, values_ref, signs_ref, mid, a)
        return carry

    lax.fori_loop(0, outer, step, 0)
    second_pass(outer, inner, cols, mid, parts)
    other = jnp.dot(parts[...], hadamard_rows(LOW), preferred_element_type=jnp.float32)
    core = lax.axis_index("narrow") & 1
    flip = (1 - 2 * core).astype(jnp.float32)
    mine = mine_ref[...]
    even_ref[...] = two_parts(other + flip * mine)
    odd_ref[...] = two_parts(mine - flip * other)


def split_groups(groups):
    outer = 1 << (groups.bit_length() - 1) // 2
    return outer, groups // outer


def transform_own(values, signs, samples):
    cols, rows = values.shape
    groups = rows // LOW
    outer, inner = split_groups(groups)
    hbm = pl.BlockSpec(memory_space=pltpu.HBM)
    return pl.pallas_call(
        functools.partial(own_kernel, outer, inner),
        out_shape=[
            jax.ShapeDtypeStruct((groups * cols, LOW), jnp.float32),
            jax.ShapeDtypeStruct(samples.shape, samples.dtype),
        ],
        in_specs=[hbm, hbm, vmem()],
        out_specs=[vmem()] * 2,
        scratch_shapes=[
            pltpu.VMEM(values.shape, jnp.float32),
            pltpu.VMEM((rows // LANES, LANES), jnp.int32),
            pltpu.VMEM((groups * cols, LOW), jnp.float32),
            pltpu.VMEM((groups * cols, 2 * LOW), jnp.bfloat16),
            pltpu.SemaphoreType.DMA((outer + 1,)),
        ],
        compiler_params=pltpu.CompilerParams(vmem_limit_bytes=VMEM_LIMIT),
        cost_estimate=pl.CostEstimate(flops=4 * cols * rows * LOW, bytes_accessed=10 * cols * rows, transcendentals=0),
        name="transform_own",
    )(
        pltpu.with_memory_space_constraint(values, pltpu.HBM),
        pltpu.with_memory_space_constraint(signs.reshape(rows // LANES, LANES), pltpu.HBM),
        samples,
    )


def transform_other(values, signs, mine):
    cols, rows = values.shape
    groups = rows // LOW
    outer, inner = split_groups(groups)
    return pl.pallas_call(
        functools.partial(other_kernel, outer, inner),
        out_shape=[jax.ShapeDtypeStruct((groups * cols, 2 * LOW), jnp.bfloat16)] * 2,
        in_specs=[vmem()] * 3,
        out_specs=[vmem()] * 2,
        scratch_shapes=[
            pltpu.VMEM((groups * cols, LOW), jnp.float32),
            pltpu.VMEM((groups * cols, 2 * LOW), jnp.bfloat16),
        ],
        compiler_params=pltpu.CompilerParams(vmem_limit_bytes=VMEM_LIMIT),
        cost_estimate=pl.CostEstimate(flops=4 * cols * rows * LOW, bytes_accessed=10 * cols * rows, transcendentals=0),
        name="transform_other",
    )(values, signs.reshape(rows // LANES, LANES), mine)


def gather_kernel(first, groups, cols, even_ref, odd_ref, offsets_ref, out_ref):
    count = offsets_ref.shape[0]
    offsets = offsets_ref[...]
    samp = offsets.shape[1]
    by_parity = [[t for t in range(count) if parity(first + t) == p] for p in range(2)]
    for table_ref, targets in zip((even_ref, odd_ref), by_parity):
        for at in range(0, len(targets), 2):
            pair = targets[at : at + 2]
            offset = jnp.concatenate([offsets[t : t + 1] for t in pair], axis=1)
            width = offset.shape[1]
            low = offset & (LOW - 1)
            high = jnp.broadcast_to(offset // LOW & (groups - 1), (cols, width))
            rows = lax.broadcasted_iota(jnp.int32, (LOW, width), 0)
            chosen = (rows == low).astype(jnp.float32).astype(jnp.bfloat16)
            chosen = jnp.concatenate([chosen, chosen], axis=0)
            picked = jnp.dot(table_ref[...], chosen, preferred_element_type=jnp.float32)
            sums = [jnp.zeros((cols, width), jnp.float32) for _ in range(2)]
            outer, inner = split_groups(groups)
            for g in range(groups):
                block = picked[g * cols : (g + 1) * cols]
                sums[g % 2] = jnp.where(high == g % outer * inner + g // outer, block, sums[g % 2])
            total = sums[0] + sums[1]
            for i, t in enumerate(pair):
                out_ref[t] = total[:, i * samp : (i + 1) * samp]


def gather(first, cols, groups, even, odd, offsets):
    count, samp = offsets.shape
    return pl.pallas_call(
        functools.partial(gather_kernel, first, groups, cols),
        out_shape=jax.ShapeDtypeStruct((count, cols, samp), jnp.float32),
        in_specs=[vmem()] * 3,
        out_specs=vmem(),
        compiler_params=pltpu.CompilerParams(vmem_limit_bytes=VMEM_LIMIT),
        cost_estimate=pl.CostEstimate(
            flops=4 * groups * cols * LOW * count * samp, bytes_accessed=4 * groups * cols * LOW, transcendentals=0
        ),
        name="gather",
    )(even, odd, offsets)


def per_device(panel, signs, samples):
    cols, rows = panel.shape
    samp = samples.shape[0]
    n_wide = lax.axis_size("wide")
    n_narrow = lax.axis_size("narrow")
    wide_bits = n_wide.bit_length() - 1
    narrow_bits = n_narrow.bit_length() - 1
    n_all = n_wide * n_narrow
    wide_me = lax.axis_index("wide")
    narrow_me = lax.axis_index("narrow")

    def across(values, mask):
        return lax.ppermute(values, AXES, [(i, i ^ mask) for i in range(n_all)])

    for bit in range(1, narrow_bits):
        if bit == 1:
            panel = panel * signs.astype(jnp.float32)[None, :]
            signs = jnp.ones_like(signs)
        upper = narrow_me >> bit & 1 == 1
        partner = across(panel, 1 << bit)
        panel = jnp.where(upper, partner - panel, panel + partner)

    groups = rows // LOW
    half = n_wide // 2
    arrived = across(samples, n_narrow | 1)
    other, other_signs = across(panel, 1), across(signs, 1)
    mine, listed = transform_own(panel, signs, samples)
    arrived, mine, listed, other, other_signs = lax.optimization_barrier((arrived, mine, listed, other, other_signs))
    asked = jnp.concatenate([listed, arrived])
    for bit in range(1, wide_bits):
        if bit == 2:
            asked, even, odd = lax.optimization_barrier((asked, even, odd))
        if bit == wide_bits - 1:
            near = gather(0, cols, groups, even, odd, asked.reshape(half, samp))
        arrived = across(asked, n_narrow << bit | 1)
        if bit == 1:
            even, odd = transform_other(other, other_signs, mine)
        asked = jnp.concatenate([asked, arrived])
    asked, near = lax.optimization_barrier((asked, near))
    asked = asked.reshape(n_wide, samp)

    far = gather(half, cols, groups, even, odd, asked[half:])
    for bit in reversed(range(wide_bits)):
        sign = (1 - 2 * (wide_me >> bit & 1)).astype(jnp.float32)
        total = across(far, n_narrow << bit | 1) + sign * near
        near, far = total[: 1 << bit >> 1], total[1 << bit >> 1 :]
    return total[0] * jnp.float32(1.0 / math.sqrt(samp * n_all))


def solution(mesh):
    in_specs = (P(None, AXES), P(AXES), P(AXES))
    return jax.shard_map(per_device, mesh=mesh, in_specs=in_specs, out_specs=P(None, AXES), check_vma=False)
```

```python
import functools
import math

import jax
import jax.numpy as jnp
from jax import lax
from jax.experimental import pallas as pl
from jax.experimental.pallas import tpu as pltpu
from jax.sharding import PartitionSpec as P

LANES = 128
LOW = 256
MIX_ROWS = 64
AXES = ("wide", "narrow")
VMEM_LIMIT = 40 << 20


def vmem():
    return pl.BlockSpec(memory_space=pltpu.VMEM)


def parity(value):
    return bin(value).count("1") & 1


def hadamard_rows(order):
    row = lax.broadcasted_iota(jnp.int32, (order, order), 0)
    col = lax.broadcasted_iota(jnp.int32, (order, order), 1)
    bits = row & col
    shift = order.bit_length() // 2
    while shift:
        bits = bits ^ (bits >> shift)
        shift //= 2
    sign = (1 - 2 * (bits & 1)).astype(jnp.float32).astype(jnp.bfloat16)
    return jnp.concatenate([sign, sign], axis=0)


def two_parts(values):
    high = values.astype(jnp.bfloat16)
    low = (values - high.astype(jnp.float32)).astype(jnp.bfloat16)
    return jnp.concatenate([high, low], axis=1)


def butterfly(values):
    values = list(values)
    step = 1
    while step < len(values):
        for at in range(len(values)):
            if not at & step:
                first, second = values[at], values[at | step]
                values[at], values[at | step] = first + second, first - second
        step *= 2
    return values


def first_pass(outer, inner, values_ref, signs_ref, mid, a):
    cols = values_ref.shape[0]
    tiles = LOW // LANES
    for tile in range(tiles):
        values = []
        for b in range(inner):
            at = (a * inner + b) * tiles + tile
            lanes = pl.ds(pl.multiple_of(at * LANES, LANES), LANES)
            values.append(values_ref[:, lanes] * signs_ref[pl.ds(at, 1), :].astype(jnp.float32))
        for b, value in enumerate(butterfly(values)):
            rows = pl.ds(pl.multiple_of((a * inner + b) * cols, cols), cols)
            mid[rows, tile * LANES : (tile + 1) * LANES] = value


def second_pass(outer, inner, cols, mid, parts):
    def step(b, carry):
        values = [mid[pl.ds(pl.multiple_of((a * inner + b) * cols, cols), cols), :] for a in range(outer)]
        block = two_parts(jnp.concatenate(butterfly(values), axis=0))
        parts[pl.ds(pl.multiple_of(b * outer * cols, outer * cols), outer * cols), :] = block
        return carry

    lax.fori_loop(0, inner, step, 0)


def high_kernel(outer, inner, values_hbm, signs_hbm, samples_ref, parts_ref, list_ref, values_ref, signs_ref, mid, sems):
    cols, rows = values_hbm.shape
    block = rows // outer
    signs_copy = pltpu.make_async_copy(signs_hbm, signs_ref, sems.at[outer])
    copies = [
        pltpu.make_async_copy(
            values_hbm.at[:, pl.ds(a * block, block)], values_ref.at[:, pl.ds(a * block, block)], sems.at[a]
        )
        for a in range(outer)
    ]
    signs_copy.start()
    for copy in copies:
        copy.start()
    list_ref[...] = samples_ref[...]
    signs_copy.wait()
    for a, copy in enumerate(copies):
        copy.wait()
        first_pass(outer, inner, values_ref, signs_ref, mid, a)
    second_pass(outer, inner, cols, mid, parts_ref)


def low_kernel(parts_ref, out_ref):
    out_ref[...] = jnp.dot(parts_ref[...], hadamard_rows(LOW), preferred_element_type=jnp.float32)


def mix_kernel(groups, mine_ref, other_ref, offsets_ref, even_ref, odd_ref, out_ref):
    core = lax.axis_index("narrow") & 1
    flip = (1 - 2 * core).astype(jnp.float32)

    def step(at, carry):
        rows = pl.ds(pl.multiple_of(at * MIX_ROWS, MIX_ROWS), MIX_ROWS)
        mine, other = mine_ref[rows, :], other_ref[rows, :]
        even_ref[rows, :] = two_parts(other + flip * mine)
        odd_ref[rows, :] = two_parts(mine - flip * other)
        return carry

    lax.fori_loop(0, mine_ref.shape[0] // MIX_ROWS, step, 0)
    pick(0, groups, mine_ref.shape[0] // groups, (even_ref, odd_ref), offsets_ref[...], out_ref, 0)


def split_groups(groups):
    outer = 1 << (groups.bit_length() - 1) // 2
    return outer, groups // outer


def transform_high(values, signs, samples):
    cols, rows = values.shape
    groups = rows // LOW
    outer, inner = split_groups(groups)
    hbm = pl.BlockSpec(memory_space=pltpu.HBM)
    return pl.pallas_call(
        functools.partial(high_kernel, outer, inner),
        out_shape=[
            jax.ShapeDtypeStruct((groups * cols, 2 * LOW), jnp.bfloat16),
            jax.ShapeDtypeStruct(samples.shape, samples.dtype),
        ],
        in_specs=[hbm, hbm, vmem()],
        out_specs=[vmem()] * 2,
        scratch_shapes=[
            pltpu.VMEM(values.shape, jnp.float32),
            pltpu.VMEM((rows // LANES, LANES), jnp.int32),
            pltpu.VMEM((groups * cols, LOW), jnp.float32),
            pltpu.SemaphoreType.DMA((outer + 1,)),
        ],
        compiler_params=pltpu.CompilerParams(vmem_limit_bytes=VMEM_LIMIT),
        cost_estimate=pl.CostEstimate(flops=4 * cols * rows * LOW, bytes_accessed=10 * cols * rows, transcendentals=0),
        name="transform_high",
    )(
        pltpu.with_memory_space_constraint(values, pltpu.HBM),
        pltpu.with_memory_space_constraint(signs.reshape(rows // LANES, LANES), pltpu.HBM),
        samples,
    )


def transform_low(parts):
    rows, width = parts.shape
    return pl.pallas_call(
        low_kernel,
        out_shape=jax.ShapeDtypeStruct((rows, width // 2), jnp.float32),
        in_specs=[vmem()],
        out_specs=vmem(),
        compiler_params=pltpu.CompilerParams(vmem_limit_bytes=VMEM_LIMIT),
        cost_estimate=pl.CostEstimate(flops=rows * width * width, bytes_accessed=4 * rows * width, transcendentals=0),
        name="transform_low",
    )(parts)


def mix(mine, other, groups, offsets):
    rows, low = mine.shape
    count, samp = offsets.shape
    return pl.pallas_call(
        functools.partial(mix_kernel, groups),
        out_shape=[
            jax.ShapeDtypeStruct((rows, 2 * low), jnp.bfloat16),
            jax.ShapeDtypeStruct((rows, 2 * low), jnp.bfloat16),
            jax.ShapeDtypeStruct((count, rows // groups, samp), jnp.float32),
        ],
        in_specs=[vmem()] * 3,
        out_specs=[vmem()] * 3,
        compiler_params=pltpu.CompilerParams(vmem_limit_bytes=VMEM_LIMIT),
        cost_estimate=pl.CostEstimate(
            flops=4 * rows * low * count * samp, bytes_accessed=16 * rows * low, transcendentals=0
        ),
        name="mix",
    )(mine, other, offsets)


def pick(first, groups, cols, tables, offsets, out_ref, at_row):
    count, samp = offsets.shape
    outer, inner = split_groups(groups)
    by_parity = [[t for t in range(count) if parity(first + t) == p] for p in range(2)]
    for table_ref, targets in zip(tables, by_parity):
        for at in range(0, len(targets), 2):
            pair = targets[at : at + 2]
            offset = jnp.concatenate([offsets[t : t + 1] for t in pair], axis=1)
            width = offset.shape[1]
            low = offset & (LOW - 1)
            high = jnp.broadcast_to(offset // LOW & (groups - 1), (cols, width))
            rows = lax.broadcasted_iota(jnp.int32, (LOW, width), 0)
            chosen = (rows == low).astype(jnp.float32).astype(jnp.bfloat16)
            chosen = jnp.concatenate([chosen, chosen], axis=0)
            picked = jnp.dot(table_ref[...], chosen, preferred_element_type=jnp.float32)
            sums = [jnp.zeros((cols, width), jnp.float32) for _ in range(2)]
            for g in range(groups):
                block = picked[g * cols : (g + 1) * cols]
                sums[g % 2] = jnp.where(high == g % outer * inner + g // outer, block, sums[g % 2])
            total = sums[0] + sums[1]
            for i, t in enumerate(pair):
                out_ref[at_row + t] = total[:, i * samp : (i + 1) * samp]


def gather_kernel(first, groups, even_ref, odd_ref, offsets_ref, known_ref, out_ref):
    kept, cols, _ = known_ref.shape
    out_ref[:kept] = known_ref[...]
    pick(first, groups, cols, (even_ref, odd_ref), offsets_ref[...], out_ref, kept)


def gather(first, groups, even, odd, offsets, known):
    count, samp = offsets.shape
    kept, cols, _ = known.shape
    return pl.pallas_call(
        functools.partial(gather_kernel, first, groups),
        out_shape=jax.ShapeDtypeStruct((kept + count, cols, samp), jnp.float32),
        in_specs=[vmem()] * 4,
        out_specs=vmem(),
        compiler_params=pltpu.CompilerParams(vmem_limit_bytes=VMEM_LIMIT),
        cost_estimate=pl.CostEstimate(
            flops=4 * groups * cols * LOW * count * samp, bytes_accessed=4 * groups * cols * LOW, transcendentals=0
        ),
        name="gather",
    )(even, odd, offsets, known)


def per_device(panel, signs, samples):
    cols, rows = panel.shape
    samp = samples.shape[0]
    n_wide = lax.axis_size("wide")
    n_narrow = lax.axis_size("narrow")
    wide_bits = n_wide.bit_length() - 1
    narrow_bits = n_narrow.bit_length() - 1
    n_all = n_wide * n_narrow
    wide_me = lax.axis_index("wide")
    narrow_me = lax.axis_index("narrow")

    def across(values, mask):
        return lax.ppermute(values, AXES, [(i, i ^ mask) for i in range(n_all)])

    for bit in range(1, narrow_bits):
        if bit == 1:
            panel = panel * signs.astype(jnp.float32)[None, :]
            signs = jnp.ones_like(signs)
        upper = narrow_me >> bit & 1 == 1
        partner = across(panel, 1 << bit)
        panel = jnp.where(upper, partner - panel, panel + partner)

    groups = rows // LOW
    half, quarter = n_wide // 2, n_wide // 4
    ladder = list(reversed(range(wide_bits)))

    def exchange(values, i):
        return across(values, n_narrow << ladder[i] | 1)

    arrived = exchange(samples, 0)
    parts, listed = transform_high(panel, signs, samples)
    arrived, parts, listed = lax.optimization_barrier((arrived, parts, listed))
    asked = jnp.concatenate([listed, arrived])
    for i in range(1, wide_bits):
        if i == 2:
            asked, mine = lax.optimization_barrier((asked, mine))
            other = across(mine, 1)
        if i == wide_bits - 1:
            asked, other = lax.optimization_barrier((asked, other))
            even, odd, early = mix(mine, other, groups, asked.reshape(half, samp))
        arrived = exchange(asked, i)
        if i == 1:
            mine = transform_low(parts)
        asked = jnp.concatenate([asked, arrived])
    arrived, early = lax.optimization_barrier((arrived, early))
    late = arrived.reshape(half, samp)

    far = gather(half + quarter, groups, even, odd, late[quarter:], early[quarter:])
    near = gather(half, groups, even, odd, late[:quarter], early[:quarter])
    for i in [wide_bits - 2, wide_bits - 1, *reversed(range(wide_bits - 2))]:
        sign = (1 - 2 * (wide_me >> ladder[i] & 1)).astype(jnp.float32)
        total = exchange(far, i) + sign * near
        middle = total.shape[0] // 2
        near, far = total[:middle], total[middle:]
    return total[0] * jnp.float32(1.0 / math.sqrt(samp * n_all))


def solution(mesh):
    in_specs = (P(None, AXES), P(AXES), P(AXES))
    return jax.shard_map(per_device, mesh=mesh, in_specs=in_specs, out_specs=P(None, AXES), check_vma=False)
```

```python
import functools
import math

import jax
import jax.numpy as jnp
from jax import lax
from jax.experimental import pallas as pl
from jax.experimental.pallas import tpu as pltpu
from jax.sharding import PartitionSpec as P

LANES = 128
LOW = 256
MIX_ROWS = 64
AXES = ("wide", "narrow")
VMEM_LIMIT = 40 << 20


def vmem():
    return pl.BlockSpec(memory_space=pltpu.VMEM)


def parity(value):
    return bin(value).count("1") & 1


def ladder_place(place, bits):
    return sum((place >> i & 1) << (bits - 1 - i) for i in range(bits))


def hadamard_rows(order):
    row = lax.broadcasted_iota(jnp.int32, (order, order), 0)
    col = lax.broadcasted_iota(jnp.int32, (order, order), 1)
    bits = row & col
    shift = order.bit_length() // 2
    while shift:
        bits = bits ^ (bits >> shift)
        shift //= 2
    sign = (1 - 2 * (bits & 1)).astype(jnp.float32).astype(jnp.bfloat16)
    return jnp.concatenate([sign, sign], axis=0)


def two_parts(values):
    high = values.astype(jnp.bfloat16)
    low = (values - high.astype(jnp.float32)).astype(jnp.bfloat16)
    return jnp.concatenate([high, low], axis=1)


def butterfly(values):
    values = list(values)
    step = 1
    while step < len(values):
        for at in range(len(values)):
            if not at & step:
                first, second = values[at], values[at | step]
                values[at], values[at | step] = first + second, first - second
        step *= 2
    return values


def first_pass(outer, inner, values_ref, signs_ref, mid, a):
    cols = values_ref.shape[0]
    tiles = LOW // LANES
    for tile in range(tiles):
        values = []
        for b in range(inner):
            at = (a * inner + b) * tiles + tile
            lanes = pl.ds(pl.multiple_of(at * LANES, LANES), LANES)
            values.append(values_ref[:, lanes] * signs_ref[pl.ds(at, 1), :].astype(jnp.float32))
        for b, value in enumerate(butterfly(values)):
            rows = pl.ds(pl.multiple_of((a * inner + b) * cols, cols), cols)
            mid[rows, tile * LANES : (tile + 1) * LANES] = value


def second_pass(outer, inner, cols, mid, parts):
    def step(b, carry):
        values = [mid[pl.ds(pl.multiple_of((a * inner + b) * cols, cols), cols), :] for a in range(outer)]
        block = two_parts(jnp.concatenate(butterfly(values), axis=0))
        parts[pl.ds(pl.multiple_of(b * outer * cols, outer * cols), outer * cols), :] = block
        return carry

    lax.fori_loop(0, inner, step, 0)


def high_kernel(outer, inner, values_hbm, signs_hbm, samples_ref, parts_ref, list_ref, values_ref, signs_ref, mid, sems):
    cols, rows = values_hbm.shape
    block = rows // outer
    signs_copy = pltpu.make_async_copy(signs_hbm, signs_ref, sems.at[outer])
    copies = [
        pltpu.make_async_copy(
            values_hbm.at[:, pl.ds(a * block, block)], values_ref.at[:, pl.ds(a * block, block)], sems.at[a]
        )
        for a in range(outer)
    ]
    signs_copy.start()
    for copy in copies:
        copy.start()
    list_ref[...] = samples_ref[...]
    signs_copy.wait()
    for a, copy in enumerate(copies):
        copy.wait()
        first_pass(outer, inner, values_ref, signs_ref, mid, a)
    second_pass(outer, inner, cols, mid, parts_ref)


def low_kernel(parts_ref, out_ref):
    out_ref[...] = jnp.dot(parts_ref[...], hadamard_rows(LOW), preferred_element_type=jnp.float32)


def mix_kernel(groups, mine_ref, other_ref, offsets_ref, even_ref, odd_ref, out_ref):
    core = lax.axis_index("narrow") & 1
    flip = (1 - 2 * core).astype(jnp.float32)

    def step(at, carry):
        rows = pl.ds(pl.multiple_of(at * MIX_ROWS, MIX_ROWS), MIX_ROWS)
        mine, other = mine_ref[rows, :], other_ref[rows, :]
        even_ref[rows, :] = two_parts(other + flip * mine)
        odd_ref[rows, :] = two_parts(mine - flip * other)
        return carry

    lax.fori_loop(0, mine_ref.shape[0] // MIX_ROWS, step, 0)
    pick(0, groups, mine_ref.shape[0] // groups, (even_ref, odd_ref), offsets_ref[...], out_ref, 0)


def split_groups(groups):
    outer = 1 << (groups.bit_length() - 1) // 2
    return outer, groups // outer


def transform_high(values, signs, samples):
    cols, rows = values.shape
    groups = rows // LOW
    outer, inner = split_groups(groups)
    hbm = pl.BlockSpec(memory_space=pltpu.HBM)
    return pl.pallas_call(
        functools.partial(high_kernel, outer, inner),
        out_shape=[
            jax.ShapeDtypeStruct((groups * cols, 2 * LOW), jnp.bfloat16),
            jax.ShapeDtypeStruct(samples.shape, samples.dtype),
        ],
        in_specs=[hbm, hbm, vmem()],
        out_specs=[vmem()] * 2,
        scratch_shapes=[
            pltpu.VMEM(values.shape, jnp.float32),
            pltpu.VMEM((rows // LANES, LANES), jnp.int32),
            pltpu.VMEM((groups * cols, LOW), jnp.float32),
            pltpu.SemaphoreType.DMA((outer + 1,)),
        ],
        compiler_params=pltpu.CompilerParams(vmem_limit_bytes=VMEM_LIMIT),
        cost_estimate=pl.CostEstimate(flops=4 * cols * rows * LOW, bytes_accessed=10 * cols * rows, transcendentals=0),
        name="transform_high",
    )(
        pltpu.with_memory_space_constraint(values, pltpu.HBM),
        pltpu.with_memory_space_constraint(signs.reshape(rows // LANES, LANES), pltpu.HBM),
        samples,
    )


def transform_low(parts):
    rows, width = parts.shape
    return pl.pallas_call(
        low_kernel,
        out_shape=jax.ShapeDtypeStruct((rows, width // 2), jnp.float32),
        in_specs=[vmem()],
        out_specs=vmem(),
        compiler_params=pltpu.CompilerParams(vmem_limit_bytes=VMEM_LIMIT),
        cost_estimate=pl.CostEstimate(flops=rows * width * width, bytes_accessed=4 * rows * width, transcendentals=0),
        name="transform_low",
    )(parts)


def mix(mine, other, groups, offsets):
    rows, low = mine.shape
    count, samp = offsets.shape
    return pl.pallas_call(
        functools.partial(mix_kernel, groups),
        out_shape=[
            jax.ShapeDtypeStruct((rows, 2 * low), jnp.bfloat16),
            jax.ShapeDtypeStruct((rows, 2 * low), jnp.bfloat16),
            jax.ShapeDtypeStruct((count, rows // groups, samp), jnp.float32),
        ],
        in_specs=[vmem()] * 3,
        out_specs=[vmem()] * 3,
        compiler_params=pltpu.CompilerParams(vmem_limit_bytes=VMEM_LIMIT),
        cost_estimate=pl.CostEstimate(
            flops=4 * rows * low * count * samp, bytes_accessed=16 * rows * low, transcendentals=0
        ),
        name="mix",
    )(mine, other, offsets)


def pick(first, groups, cols, tables, offsets, out_ref, at_row):
    count, samp = offsets.shape
    outer, inner = split_groups(groups)
    by_parity = [[t for t in range(count) if parity(first + t) == p] for p in range(2)]
    for table_ref, targets in zip(tables, by_parity):
        for at in range(0, len(targets), 2):
            pair = targets[at : at + 2]
            offset = jnp.concatenate([offsets[t : t + 1] for t in pair], axis=1)
            width = offset.shape[1]
            low = offset & (LOW - 1)
            high = jnp.broadcast_to(offset // LOW & (groups - 1), (cols, width))
            rows = lax.broadcasted_iota(jnp.int32, (LOW, width), 0)
            chosen = (rows == low).astype(jnp.float32).astype(jnp.bfloat16)
            chosen = jnp.concatenate([chosen, chosen], axis=0)
            picked = jnp.dot(table_ref[...], chosen, preferred_element_type=jnp.float32)
            sums = [jnp.zeros((cols, width), jnp.float32) for _ in range(2)]
            for g in range(groups):
                block = picked[g * cols : (g + 1) * cols]
                sums[g % 2] = jnp.where(high == g % outer * inner + g // outer, block, sums[g % 2])
            total = sums[0] + sums[1]
            for i, t in enumerate(pair):
                out_ref[at_row + t] = total[:, i * samp : (i + 1) * samp]


def gather_kernel(first, groups, bits, turn, scale, even_ref, odd_ref, offsets_ref, known_ref, out_ref, late_ref):
    kept, cols, _ = known_ref.shape
    me = lax.axis_index("wide")

    def place(place_of, value):
        target = me ^ place_of
        common = target & me
        odd = common & 1
        for bit in range(1, bits):
            odd = odd ^ (common >> bit & 1)
        out_ref[target ^ turn] = value * ((1 - 2 * odd).astype(jnp.float32) * scale)

    pick(first, groups, cols, (even_ref, odd_ref), offsets_ref[...], late_ref, 0)
    for t in range(kept):
        place(ladder_place(t, bits), known_ref[t])
    for t in range(late_ref.shape[0]):
        place(ladder_place(first + t, bits), late_ref[t])


def gather(first, groups, bits, turn, scale, even, odd, offsets, known):
    count, samp = offsets.shape
    kept, cols, _ = known.shape
    return pl.pallas_call(
        functools.partial(gather_kernel, first, groups, bits, turn, scale),
        out_shape=jax.ShapeDtypeStruct((kept + count, cols, samp), jnp.float32),
        in_specs=[vmem()] * 4,
        out_specs=vmem(),
        scratch_shapes=[pltpu.VMEM((count, cols, samp), jnp.float32)],
        compiler_params=pltpu.CompilerParams(vmem_limit_bytes=VMEM_LIMIT),
        cost_estimate=pl.CostEstimate(
            flops=4 * groups * cols * LOW * count * samp, bytes_accessed=4 * groups * cols * LOW, transcendentals=0
        ),
        name="gather",
    )(even, odd, offsets, known)


def per_device(panel, signs, samples):
    cols, rows = panel.shape
    samp = samples.shape[0]
    n_wide = lax.axis_size("wide")
    n_narrow = lax.axis_size("narrow")
    wide_bits = n_wide.bit_length() - 1
    narrow_bits = n_narrow.bit_length() - 1
    n_all = n_wide * n_narrow
    narrow_me = lax.axis_index("narrow")

    def across(values, mask):
        return lax.ppermute(values, AXES, [(i, i ^ mask) for i in range(n_all)])

    for bit in range(1, narrow_bits):
        if bit == 1:
            panel = panel * signs.astype(jnp.float32)[None, :]
            signs = jnp.ones_like(signs)
        upper = narrow_me >> bit & 1 == 1
        partner = across(panel, 1 << bit)
        panel = jnp.where(upper, partner - panel, panel + partner)

    groups = rows // LOW
    half = n_wide // 2
    ladder = list(reversed(range(wide_bits)))

    def exchange(values, i):
        return across(values, n_narrow << ladder[i] | 1)

    arrived = exchange(samples, 0)
    parts, listed = transform_high(panel, signs, samples)
    arrived, parts, listed = lax.optimization_barrier((arrived, parts, listed))
    asked = jnp.concatenate([listed, arrived])
    for i in range(1, wide_bits):
        if i == 2:
            asked, mine = lax.optimization_barrier((asked, mine))
            other = across(mine, 1)
        if i == wide_bits - 1:
            asked, other = lax.optimization_barrier((asked, other))
            even, odd, early = mix(mine, other, groups, asked.reshape(half, samp))
        arrived = exchange(asked, i)
        if i == 1:
            mine = transform_low(parts)
        asked = jnp.concatenate([asked, arrived])
    arrived, early = lax.optimization_barrier((arrived, early))
    late = arrived.reshape(half, samp)

    scale = 1.0 / math.sqrt(samp * n_all)
    turn = n_wide - 1
    pieces = gather(half, groups, wide_bits, turn, scale, even, odd, late, early)
    teams = [[w * n_narrow + (n ^ parity(w)) for w in reversed(range(n_wide))] for n in range(n_narrow)]
    pieces = lax.all_to_all(pieces, AXES, 0, 0, axis_index_groups=teams, tiled=True)
    return jnp.sum(pieces, axis=0)


def solution(mesh):
    in_specs = (P(None, AXES), P(AXES), P(AXES))
    return jax.shard_map(per_device, mesh=mesh, in_specs=in_specs, out_specs=P(None, AXES), check_vma=False)
```

```python
import functools
import math

import jax
import jax.numpy as jnp
from jax import lax
from jax.experimental import pallas as pl
from jax.experimental.pallas import tpu as pltpu
from jax.sharding import PartitionSpec as P

LANES = 128
LOW = 256
MIX_ROWS = 64
AXES = ("wide", "narrow")
VMEM_LIMIT = 40 << 20


def vmem():
    return pl.BlockSpec(memory_space=pltpu.VMEM)


def parity(value):
    return bin(value).count("1") & 1


def ladder_place(place, bits):
    return sum((place >> i & 1) << (bits - 1 - i) for i in range(bits))


def hadamard_rows(order):
    row = lax.broadcasted_iota(jnp.int32, (order, order), 0)
    col = lax.broadcasted_iota(jnp.int32, (order, order), 1)
    bits = row & col
    shift = order.bit_length() // 2
    while shift:
        bits = bits ^ (bits >> shift)
        shift //= 2
    sign = (1 - 2 * (bits & 1)).astype(jnp.float32).astype(jnp.bfloat16)
    return jnp.concatenate([sign, sign], axis=0)


def two_parts(values):
    high = values.astype(jnp.bfloat16)
    low = (values - high.astype(jnp.float32)).astype(jnp.bfloat16)
    return jnp.concatenate([high, low], axis=1)


def butterfly(values):
    values = list(values)
    step = 1
    while step < len(values):
        for at in range(len(values)):
            if not at & step:
                first, second = values[at], values[at | step]
                values[at], values[at | step] = first + second, first - second
        step *= 2
    return values


def first_pass(outer, inner, values_ref, signs_ref, mid, a):
    cols = values_ref.shape[0]
    tiles = LOW // LANES
    for tile in range(tiles):
        values = []
        for b in range(inner):
            at = (a * inner + b) * tiles + tile
            lanes = pl.ds(pl.multiple_of(at * LANES, LANES), LANES)
            values.append(values_ref[:, lanes] * signs_ref[pl.ds(at, 1), :].astype(jnp.float32))
        for b, value in enumerate(butterfly(values)):
            rows = pl.ds(pl.multiple_of((a * inner + b) * cols, cols), cols)
            mid[rows, tile * LANES : (tile + 1) * LANES] = value


def second_pass(outer, inner, cols, mid, parts):
    def step(b, carry):
        values = [mid[pl.ds(pl.multiple_of((a * inner + b) * cols, cols), cols), :] for a in range(outer)]
        block = two_parts(jnp.concatenate(butterfly(values), axis=0))
        parts[pl.ds(pl.multiple_of(b * outer * cols, outer * cols), outer * cols), :] = block
        return carry

    lax.fori_loop(0, inner, step, 0)


def transform_kernel(outer, inner, values_hbm, signs_hbm, samples_ref, out_ref, list_ref, values_ref, signs_ref, mid, parts, sems):
    cols, rows = values_hbm.shape
    block = rows // outer
    signs_copy = pltpu.make_async_copy(signs_hbm, signs_ref, sems.at[outer])
    copies = [
        pltpu.make_async_copy(
            values_hbm.at[:, pl.ds(a * block, block)], values_ref.at[:, pl.ds(a * block, block)], sems.at[a]
        )
        for a in range(outer)
    ]
    signs_copy.start()
    for copy in copies:
        copy.start()
    list_ref[...] = samples_ref[...]
    matrix = hadamard_rows(LOW)
    signs_copy.wait()
    for a, copy in enumerate(copies):
        copy.wait()
        first_pass(outer, inner, values_ref, signs_ref, mid, a)
    second_pass(outer, inner, cols, mid, parts)
    out_ref[...] = jnp.dot(parts[...], matrix, preferred_element_type=jnp.float32)


def mix_kernel(firsts, groups, mine_ref, other_ref, *refs):
    *offset_refs, even_ref, odd_ref, out_ref = refs
    core = lax.axis_index("narrow") & 1
    flip = (1 - 2 * core).astype(jnp.float32)

    def step(at, carry):
        rows = pl.ds(pl.multiple_of(at * MIX_ROWS, MIX_ROWS), MIX_ROWS)
        mine, other = mine_ref[rows, :], other_ref[rows, :]
        even_ref[rows, :] = two_parts(other + flip * mine)
        odd_ref[rows, :] = two_parts(mine - flip * other)
        return carry

    lax.fori_loop(0, mine_ref.shape[0] // MIX_ROWS, step, 0)
    at_row = 0
    for first, offsets_ref in zip(firsts, offset_refs):
        pick(first, groups, mine_ref.shape[0] // groups, (even_ref, odd_ref), offsets_ref[...], out_ref, at_row)
        at_row += offsets_ref.shape[0]


def split_groups(groups):
    outer = 1 << (groups.bit_length() - 1) // 2
    return outer, groups // outer


def transform(values, signs, samples):
    cols, rows = values.shape
    groups = rows // LOW
    outer, inner = split_groups(groups)
    hbm = pl.BlockSpec(memory_space=pltpu.HBM)
    return pl.pallas_call(
        functools.partial(transform_kernel, outer, inner),
        out_shape=[
            jax.ShapeDtypeStruct((groups * cols, LOW), jnp.float32),
            jax.ShapeDtypeStruct(samples.shape, samples.dtype),
        ],
        in_specs=[hbm, hbm, vmem()],
        out_specs=[vmem()] * 2,
        scratch_shapes=[
            pltpu.VMEM(values.shape, jnp.float32),
            pltpu.VMEM((rows // LANES, LANES), jnp.int32),
            pltpu.VMEM((groups * cols, LOW), jnp.float32),
            pltpu.VMEM((groups * cols, 2 * LOW), jnp.bfloat16),
            pltpu.SemaphoreType.DMA((outer + 1,)),
        ],
        compiler_params=pltpu.CompilerParams(vmem_limit_bytes=VMEM_LIMIT),
        cost_estimate=pl.CostEstimate(flops=4 * cols * rows * LOW, bytes_accessed=10 * cols * rows, transcendentals=0),
        name="transform",
    )(
        pltpu.with_memory_space_constraint(values, pltpu.HBM),
        pltpu.with_memory_space_constraint(signs.reshape(rows // LANES, LANES), pltpu.HBM),
        samples,
    )


def gather_cost(groups, cols, count, samp):
    return pl.CostEstimate(
        flops=4 * groups * cols * LOW * count * samp, bytes_accessed=4 * groups * cols * LOW, transcendentals=0
    )


def mix(firsts, groups, mine, other, lists):
    rows, low = mine.shape
    count, samp = sum(offsets.shape[0] for offsets in lists), lists[0].shape[1]
    return pl.pallas_call(
        functools.partial(mix_kernel, firsts, groups),
        out_shape=[
            jax.ShapeDtypeStruct((rows, 2 * low), jnp.bfloat16),
            jax.ShapeDtypeStruct((rows, 2 * low), jnp.bfloat16),
            jax.ShapeDtypeStruct((count, rows // groups, samp), jnp.float32),
        ],
        in_specs=[vmem()] * (2 + len(lists)),
        out_specs=[vmem()] * 3,
        compiler_params=pltpu.CompilerParams(vmem_limit_bytes=VMEM_LIMIT),
        cost_estimate=gather_cost(groups, rows // groups, count, samp),
        name="mix",
    )(mine, other, *lists)


def pick(first, groups, cols, tables, offsets, out_ref, at_row):
    count, samp = offsets.shape
    outer, inner = split_groups(groups)
    by_parity = [[t for t in range(count) if parity(first + t) == p] for p in range(2)]
    for table_ref, targets in zip(tables, by_parity):
        for at in range(0, len(targets), 2):
            pair = targets[at : at + 2]
            offset = jnp.concatenate([offsets[t : t + 1] for t in pair], axis=1)
            width = offset.shape[1]
            low = offset & (LOW - 1)
            high = jnp.broadcast_to(offset // LOW & (groups - 1), (cols, width))
            rows = lax.broadcasted_iota(jnp.int32, (LOW, width), 0)
            chosen = (rows == low).astype(jnp.float32).astype(jnp.bfloat16)
            chosen = jnp.concatenate([chosen, chosen], axis=0)
            picked = jnp.dot(table_ref[...], chosen, preferred_element_type=jnp.float32)
            sums = [jnp.zeros((cols, width), jnp.float32) for _ in range(2)]
            for g in range(groups):
                block = picked[g * cols : (g + 1) * cols]
                sums[g % 2] = jnp.where(high == g % outer * inner + g // outer, block, sums[g % 2])
            total = sums[0] + sums[1]
            for i, t in enumerate(pair):
                out_ref[at_row + t] = total[:, i * samp : (i + 1) * samp]


def early_kernel(firsts, groups, even_ref, odd_ref, *refs):
    *offset_refs, out_ref = refs
    at_row = 0
    for first, offsets_ref in zip(firsts, offset_refs):
        pick(first, groups, out_ref.shape[1], (even_ref, odd_ref), offsets_ref[...], out_ref, at_row)
        at_row += offsets_ref.shape[0]


def gather_kernel(first, groups, bits, first_piece, scale, even_ref, odd_ref, offsets_ref, *refs):
    *known_refs, out_ref, late_ref = refs
    cols = out_ref.shape[1]
    me = lax.axis_index("wide")

    def place(place_of, value):
        target = me ^ place_of
        common = target & me
        odd = common & 1
        for bit in range(1, bits):
            odd = odd ^ (common >> bit & 1)
        out_ref[target - first_piece & (1 << bits) - 1] = value * ((1 - 2 * odd).astype(jnp.float32) * scale)

    pick(first, groups, cols, (even_ref, odd_ref), offsets_ref[...], late_ref, 0)
    at_place = 0
    for ref in (*known_refs, late_ref):
        for t in range(ref.shape[0]):
            place(ladder_place(at_place, bits), ref[t])
            at_place += 1


def gather_early(firsts, groups, even, odd, lists):
    count, samp = sum(offsets.shape[0] for offsets in lists), lists[0].shape[1]
    cols = even.shape[0] // groups
    return pl.pallas_call(
        functools.partial(early_kernel, firsts, groups),
        out_shape=jax.ShapeDtypeStruct((count, cols, samp), jnp.float32),
        in_specs=[vmem()] * (2 + len(lists)),
        out_specs=vmem(),
        compiler_params=pltpu.CompilerParams(vmem_limit_bytes=VMEM_LIMIT),
        cost_estimate=gather_cost(groups, cols, count, samp),
        name="gather_early",
    )(even, odd, *lists)


def gather(first, groups, bits, first_piece, scale, even, odd, offsets, known):
    count, samp = offsets.shape
    cols = even.shape[0] // groups
    return pl.pallas_call(
        functools.partial(gather_kernel, first, groups, bits, first_piece, scale),
        out_shape=jax.ShapeDtypeStruct((first + count, cols, samp), jnp.float32),
        in_specs=[vmem()] * (3 + len(known)),
        out_specs=vmem(),
        scratch_shapes=[pltpu.VMEM((count, cols, samp), jnp.float32)],
        compiler_params=pltpu.CompilerParams(vmem_limit_bytes=VMEM_LIMIT),
        cost_estimate=gather_cost(groups, cols, count, samp),
        name="gather",
    )(even, odd, offsets, *known)


def per_device(panel, signs, samples):
    cols, rows = panel.shape
    samp = samples.shape[0]
    n_wide = lax.axis_size("wide")
    n_narrow = lax.axis_size("narrow")
    wide_bits = n_wide.bit_length() - 1
    narrow_bits = n_narrow.bit_length() - 1
    n_all = n_wide * n_narrow
    narrow_me = lax.axis_index("narrow")

    def across(values, mask):
        return lax.ppermute(values, AXES, [(i, i ^ mask) for i in range(n_all)])

    for bit in range(1, narrow_bits):
        if bit == 1:
            panel = panel * signs.astype(jnp.float32)[None, :]
            signs = jnp.ones_like(signs)
        upper = narrow_me >> bit & 1 == 1
        partner = across(panel, 1 << bit)
        panel = jnp.where(upper, partner - panel, panel + partner)

    groups = rows // LOW
    half, quarter = n_wide // 2, n_wide // 4
    ladder = list(reversed(range(wide_bits)))
    last = wide_bits - 1

    def exchange(values, i):
        return across(values, n_narrow << ladder[i] | 1)

    arrived = exchange(samples, 0)
    mine, listed = transform(panel, signs, samples)
    arrived, mine, listed = lax.optimization_barrier((arrived, mine, listed))
    other = across(mine, 1)
    asked = jnp.concatenate([listed, arrived])
    for i in range(1, last - 1):
        asked = jnp.concatenate([asked, exchange(asked, i)])
    arrived = exchange(asked, last - 1)
    even, odd, early = mix((0,), groups, mine, other, [asked.reshape(quarter, samp)])
    asked, arrived, even, odd, early = lax.optimization_barrier((asked, arrived, even, odd, early))
    late = exchange(jnp.concatenate([asked, arrived]), last)
    early = [early, gather_early((quarter,), groups, even, odd, [arrived.reshape(quarter, samp)])]
    late, *early = lax.optimization_barrier((late, *early))
    late = late.reshape(half, samp)

    scale = 1.0 / math.sqrt(samp * n_all)
    first_piece = n_wide * 11 // 16
    pieces = gather(half, groups, wide_bits, first_piece, scale, even, odd, late, early)
    order = [(p + first_piece) % n_wide for p in range(n_wide)]
    teams = [[w * n_narrow + (n ^ parity(w)) for w in order] for n in range(n_narrow)]
    pieces = lax.all_to_all(pieces, AXES, 0, 0, axis_index_groups=teams, tiled=True)
    return jnp.sum(pieces, axis=0)


def solution(mesh):
    in_specs = (P(None, AXES), P(AXES), P(AXES))
    return jax.shard_map(per_device, mesh=mesh, in_specs=in_specs, out_specs=P(None, AXES), check_vma=False)
```

```python
import functools
import math

import jax
import jax.numpy as jnp
from jax import lax
from jax.experimental import pallas as pl
from jax.experimental.pallas import tpu as pltpu
from jax.sharding import PartitionSpec as P

LANES = 128
LOW = 256
MIX_ROWS = 64
AXES = ("wide", "narrow")
VMEM_LIMIT = 40 << 20


def vmem():
    return pl.BlockSpec(memory_space=pltpu.VMEM)


def parity(value):
    return bin(value).count("1") & 1


def ladder_place(place, bits):
    return sum((place >> i & 1) << (bits - 1 - i) for i in range(bits))


def hadamard_rows(order):
    row = lax.broadcasted_iota(jnp.int32, (order, order), 0)
    col = lax.broadcasted_iota(jnp.int32, (order, order), 1)
    bits = row & col
    shift = order.bit_length() // 2
    while shift:
        bits = bits ^ (bits >> shift)
        shift //= 2
    sign = (1 - 2 * (bits & 1)).astype(jnp.float32).astype(jnp.bfloat16)
    return jnp.concatenate([sign, sign], axis=0)


def two_parts(values):
    high = values.astype(jnp.bfloat16)
    low = (values - high.astype(jnp.float32)).astype(jnp.bfloat16)
    return jnp.concatenate([high, low], axis=1)


def butterfly(values):
    values = list(values)
    step = 1
    while step < len(values):
        for at in range(len(values)):
            if not at & step:
                first, second = values[at], values[at | step]
                values[at], values[at | step] = first + second, first - second
        step *= 2
    return values


def first_pass(outer, inner, values_ref, signs_ref, mid, a):
    cols = values_ref.shape[0]
    tiles = LOW // LANES
    for tile in range(tiles):
        values = []
        for b in range(inner):
            at = (a * inner + b) * tiles + tile
            lanes = pl.ds(pl.multiple_of(at * LANES, LANES), LANES)
            values.append(values_ref[:, lanes] * signs_ref[pl.ds(at, 1), :].astype(jnp.float32))
        for b, value in enumerate(butterfly(values)):
            rows = pl.ds(pl.multiple_of((a * inner + b) * cols, cols), cols)
            mid[rows, tile * LANES : (tile + 1) * LANES] = value


def second_pass(outer, inner, cols, mid, parts):
    def step(b, carry):
        values = [mid[pl.ds(pl.multiple_of((a * inner + b) * cols, cols), cols), :] for a in range(outer)]
        block = two_parts(jnp.concatenate(butterfly(values), axis=0))
        parts[pl.ds(pl.multiple_of(b * outer * cols, outer * cols), outer * cols), :] = block
        return carry

    lax.fori_loop(0, inner, step, 0)


def transform_kernel(outer, inner, values_hbm, signs_hbm, samples_ref, out_ref, list_ref, values_ref, signs_ref, mid, parts, sems):
    cols, rows = values_hbm.shape
    block = rows // outer
    signs_copy = pltpu.make_async_copy(signs_hbm, signs_ref, sems.at[outer])
    copies = [
        pltpu.make_async_copy(
            values_hbm.at[:, pl.ds(a * block, block)], values_ref.at[:, pl.ds(a * block, block)], sems.at[a]
        )
        for a in range(outer)
    ]
    signs_copy.start()
    for copy in copies:
        copy.start()
    list_ref[...] = samples_ref[...]
    matrix = hadamard_rows(LOW)
    signs_copy.wait()
    for a, copy in enumerate(copies):
        copy.wait()
        first_pass(outer, inner, values_ref, signs_ref, mid, a)
    second_pass(outer, inner, cols, mid, parts)
    out_ref[...] = jnp.dot(parts[...], matrix, preferred_element_type=jnp.float32)


def mix_kernel(mine_ref, other_ref, even_ref, odd_ref):
    core = lax.axis_index("narrow") & 1
    flip = (1 - 2 * core).astype(jnp.float32)

    def step(at, carry):
        rows = pl.ds(pl.multiple_of(at * MIX_ROWS, MIX_ROWS), MIX_ROWS)
        mine, other = mine_ref[rows, :], other_ref[rows, :]
        even_ref[rows, :] = two_parts(other + flip * mine)
        odd_ref[rows, :] = two_parts(mine - flip * other)
        return carry

    lax.fori_loop(0, mine_ref.shape[0] // MIX_ROWS, step, 0)


def split_groups(groups):
    outer = 1 << (groups.bit_length() - 1) // 2
    return outer, groups // outer


def transform(values, signs, samples):
    cols, rows = values.shape
    groups = rows // LOW
    outer, inner = split_groups(groups)
    hbm = pl.BlockSpec(memory_space=pltpu.HBM)
    return pl.pallas_call(
        functools.partial(transform_kernel, outer, inner),
        out_shape=[
            jax.ShapeDtypeStruct((groups * cols, LOW), jnp.float32),
            jax.ShapeDtypeStruct(samples.shape, samples.dtype),
        ],
        in_specs=[hbm, hbm, vmem()],
        out_specs=[vmem()] * 2,
        scratch_shapes=[
            pltpu.VMEM(values.shape, jnp.float32),
            pltpu.VMEM((rows // LANES, LANES), jnp.int32),
            pltpu.VMEM((groups * cols, LOW), jnp.float32),
            pltpu.VMEM((groups * cols, 2 * LOW), jnp.bfloat16),
            pltpu.SemaphoreType.DMA((outer + 1,)),
        ],
        compiler_params=pltpu.CompilerParams(vmem_limit_bytes=VMEM_LIMIT),
        cost_estimate=pl.CostEstimate(flops=4 * cols * rows * LOW, bytes_accessed=10 * cols * rows, transcendentals=0),
        name="transform",
    )(
        pltpu.with_memory_space_constraint(values, pltpu.HBM),
        pltpu.with_memory_space_constraint(signs.reshape(rows // LANES, LANES), pltpu.HBM),
        samples,
    )


def gather_cost(groups, cols, count, samp):
    return pl.CostEstimate(
        flops=4 * groups * cols * LOW * count * samp, bytes_accessed=4 * groups * cols * LOW, transcendentals=0
    )


def mix(mine, other):
    rows, low = mine.shape
    return pl.pallas_call(
        mix_kernel,
        out_shape=[jax.ShapeDtypeStruct((rows, 2 * low), jnp.bfloat16)] * 2,
        in_specs=[vmem()] * 2,
        out_specs=[vmem()] * 2,
        compiler_params=pltpu.CompilerParams(vmem_limit_bytes=VMEM_LIMIT),
        cost_estimate=pl.CostEstimate(flops=8 * rows * low, bytes_accessed=16 * rows * low, transcendentals=0),
        name="mix",
    )(mine, other)


def pick(first, groups, cols, tables, offsets, out_ref, at_row):
    count, samp = offsets.shape
    outer, inner = split_groups(groups)
    by_parity = [[t for t in range(count) if parity(first + t) == p] for p in range(2)]
    for table_ref, targets in zip(tables, by_parity):
        for at in range(0, len(targets), 2):
            pair = targets[at : at + 2]
            offset = jnp.concatenate([offsets[t : t + 1] for t in pair], axis=1)
            width = offset.shape[1]
            low = offset & (LOW - 1)
            high = jnp.broadcast_to(offset // LOW & (groups - 1), (cols, width))
            rows = lax.broadcasted_iota(jnp.int32, (LOW, width), 0)
            chosen = (rows == low).astype(jnp.float32).astype(jnp.bfloat16)
            chosen = jnp.concatenate([chosen, chosen], axis=0)
            picked = jnp.dot(table_ref[...], chosen, preferred_element_type=jnp.float32)
            sums = [jnp.zeros((cols, width), jnp.float32) for _ in range(2)]
            for g in range(groups):
                block = picked[g * cols : (g + 1) * cols]
                sums[g % 2] = jnp.where(high == g % outer * inner + g // outer, block, sums[g % 2])
            total = sums[0] + sums[1]
            for i, t in enumerate(pair):
                out_ref[at_row + t] = total[:, i * samp : (i + 1) * samp]


def early_kernel(firsts, groups, even_ref, odd_ref, *refs):
    *offset_refs, out_ref = refs
    at_row = 0
    for first, offsets_ref in zip(firsts, offset_refs):
        pick(first, groups, out_ref.shape[1], (even_ref, odd_ref), offsets_ref[...], out_ref, at_row)
        at_row += offsets_ref.shape[0]


def gather_kernel(first, groups, bits, first_piece, scale, even_ref, odd_ref, offsets_ref, *refs):
    *known_refs, out_ref, late_ref = refs
    cols = out_ref.shape[1]
    me = lax.axis_index("wide")

    def place(place_of, value):
        target = me ^ place_of
        common = target & me
        odd = common & 1
        for bit in range(1, bits):
            odd = odd ^ (common >> bit & 1)
        out_ref[target - first_piece & (1 << bits) - 1] = value * ((1 - 2 * odd).astype(jnp.float32) * scale)

    pick(first, groups, cols, (even_ref, odd_ref), offsets_ref[...], late_ref, 0)
    at_place = 0
    for ref in (*known_refs, late_ref):
        for t in range(ref.shape[0]):
            place(ladder_place(at_place, bits), ref[t])
            at_place += 1


def gather_early(firsts, groups, even, odd, lists):
    count, samp = sum(offsets.shape[0] for offsets in lists), lists[0].shape[1]
    cols = even.shape[0] // groups
    return pl.pallas_call(
        functools.partial(early_kernel, firsts, groups),
        out_shape=jax.ShapeDtypeStruct((count, cols, samp), jnp.float32),
        in_specs=[vmem()] * (2 + len(lists)),
        out_specs=vmem(),
        compiler_params=pltpu.CompilerParams(vmem_limit_bytes=VMEM_LIMIT),
        cost_estimate=gather_cost(groups, cols, count, samp),
        name="gather_early",
    )(even, odd, *lists)


def gather(first, groups, bits, first_piece, scale, even, odd, offsets, known):
    count, samp = offsets.shape
    cols = even.shape[0] // groups
    return pl.pallas_call(
        functools.partial(gather_kernel, first, groups, bits, first_piece, scale),
        out_shape=jax.ShapeDtypeStruct((first + count, cols, samp), jnp.float32),
        in_specs=[vmem()] * (3 + len(known)),
        out_specs=vmem(),
        scratch_shapes=[pltpu.VMEM((count, cols, samp), jnp.float32)],
        compiler_params=pltpu.CompilerParams(vmem_limit_bytes=VMEM_LIMIT),
        cost_estimate=gather_cost(groups, cols, count, samp),
        name="gather",
    )(even, odd, offsets, *known)


def per_device(panel, signs, samples):
    cols, rows = panel.shape
    samp = samples.shape[0]
    n_wide = lax.axis_size("wide")
    n_narrow = lax.axis_size("narrow")
    wide_bits = n_wide.bit_length() - 1
    narrow_bits = n_narrow.bit_length() - 1
    n_all = n_wide * n_narrow
    narrow_me = lax.axis_index("narrow")

    def across(values, mask):
        return lax.ppermute(values, AXES, [(i, i ^ mask) for i in range(n_all)])

    for bit in range(1, narrow_bits):
        if bit == 1:
            panel = panel * signs.astype(jnp.float32)[None, :]
            signs = jnp.ones_like(signs)
        upper = narrow_me >> bit & 1 == 1
        partner = across(panel, 1 << bit)
        panel = jnp.where(upper, partner - panel, panel + partner)

    groups = rows // LOW
    half, quarter = n_wide // 2, n_wide // 4
    ladder = list(reversed(range(wide_bits)))
    last = wide_bits - 1

    def exchange(values, i):
        return across(values, n_narrow << ladder[i] | 1)

    arrived = exchange(samples, 0)
    mine, listed = transform(panel, signs, samples)
    arrived, mine, listed = lax.optimization_barrier((arrived, mine, listed))
    other = across(mine, 1)
    asked = jnp.concatenate([listed, arrived])
    for i in range(1, last - 1):
        arrived = exchange(asked, i)
        if i == last - 2:
            even, odd = mix(mine, other)
            asked, arrived, even, odd = lax.optimization_barrier((asked, arrived, even, odd))
        asked = jnp.concatenate([asked, arrived])
    arrived = exchange(asked, last - 1)
    ahead = exchange(asked, last)
    late = exchange(arrived, last)
    lists = [asked.reshape(quarter, samp), arrived.reshape(quarter, samp), ahead.reshape(quarter, samp)]
    early = [gather_early((0, quarter, half), groups, even, odd, lists)]
    late, *early = lax.optimization_barrier((late, *early))
    late = late.reshape(quarter, samp)

    scale = 1.0 / math.sqrt(samp * n_all)
    first_piece = n_wide * 11 // 16
    pieces = gather(half + quarter, groups, wide_bits, first_piece, scale, even, odd, late, early)
    order = [(p + first_piece) % n_wide for p in range(n_wide)]
    teams = [[w * n_narrow + (n ^ parity(w)) for w in order] for n in range(n_narrow)]
    pieces = lax.all_to_all(pieces, AXES, 0, 0, axis_index_groups=teams, tiled=True)
    return jnp.sum(pieces, axis=0)


def solution(mesh):
    in_specs = (P(None, AXES), P(AXES), P(AXES))
    return jax.shard_map(per_device, mesh=mesh, in_specs=in_specs, out_specs=P(None, AXES), check_vma=False)
```

```python
import functools
import math

import jax
import jax.numpy as jnp
from jax import lax
from jax.experimental import pallas as pl
from jax.experimental.pallas import tpu as pltpu
from jax.sharding import PartitionSpec as P

LANES = 128
LOW = 256
MIX_ROWS = 64
AXES = ("wide", "narrow")
VMEM_LIMIT = 40 << 20


def vmem():
    return pl.BlockSpec(memory_space=pltpu.VMEM)


def parity(value):
    return bin(value).count("1") & 1


def ladder_place(place, bits):
    return sum((place >> i & 1) << (bits - 1 - i) for i in range(bits))


def hadamard_rows(order):
    row = lax.broadcasted_iota(jnp.int32, (order, order), 0)
    col = lax.broadcasted_iota(jnp.int32, (order, order), 1)
    bits = row & col
    shift = order.bit_length() // 2
    while shift:
        bits = bits ^ (bits >> shift)
        shift //= 2
    sign = (1 - 2 * (bits & 1)).astype(jnp.float32).astype(jnp.bfloat16)
    return jnp.concatenate([sign, sign], axis=0)


def two_parts(values):
    high = values.astype(jnp.bfloat16)
    low = (values - high.astype(jnp.float32)).astype(jnp.bfloat16)
    return jnp.concatenate([high, low], axis=1)


def butterfly(values):
    values = list(values)
    step = 1
    while step < len(values):
        for at in range(len(values)):
            if not at & step:
                first, second = values[at], values[at | step]
                values[at], values[at | step] = first + second, first - second
        step *= 2
    return values


def first_pass(outer, inner, values_ref, signs_ref, mid, a):
    cols = values_ref.shape[0]
    tiles = LOW // LANES
    for tile in range(tiles):
        values = []
        for b in range(inner):
            at = (a * inner + b) * tiles + tile
            lanes = pl.ds(pl.multiple_of(at * LANES, LANES), LANES)
            values.append(values_ref[:, lanes] * signs_ref[pl.ds(at, 1), :].astype(jnp.float32))
        for b, value in enumerate(butterfly(values)):
            rows = pl.ds(pl.multiple_of((a * inner + b) * cols, cols), cols)
            mid[rows, tile * LANES : (tile + 1) * LANES] = value


def second_pass(outer, inner, cols, mid, parts):
    def step(b, carry):
        values = [mid[pl.ds(pl.multiple_of((a * inner + b) * cols, cols), cols), :] for a in range(outer)]
        block = two_parts(jnp.concatenate(butterfly(values), axis=0))
        parts[pl.ds(pl.multiple_of(b * outer * cols, outer * cols), outer * cols), :] = block
        return carry

    lax.fori_loop(0, inner, step, 0)


def transform_kernel(outer, inner, values_hbm, signs_hbm, samples_ref, out_ref, list_ref, values_ref, signs_ref, mid, parts, sems):
    cols, rows = values_hbm.shape
    block = rows // outer
    signs_copy = pltpu.make_async_copy(signs_hbm, signs_ref, sems.at[outer])
    copies = [
        pltpu.make_async_copy(
            values_hbm.at[:, pl.ds(a * block, block)], values_ref.at[:, pl.ds(a * block, block)], sems.at[a]
        )
        for a in range(outer)
    ]
    signs_copy.start()
    for copy in copies:
        copy.start()
    list_ref[...] = samples_ref[...]
    matrix = hadamard_rows(LOW)
    signs_copy.wait()
    for a, copy in enumerate(copies):
        copy.wait()
        first_pass(outer, inner, values_ref, signs_ref, mid, a)
    second_pass(outer, inner, cols, mid, parts)
    out_ref[...] = jnp.dot(parts[...], matrix, preferred_element_type=jnp.float32)


def mix_kernel(mine_ref, other_ref, even_ref, odd_ref):
    core = lax.axis_index("narrow") & 1
    flip = (1 - 2 * core).astype(jnp.float32)

    def step(at, carry):
        rows = pl.ds(pl.multiple_of(at * MIX_ROWS, MIX_ROWS), MIX_ROWS)
        mine, other = mine_ref[rows, :], other_ref[rows, :]
        even_ref[rows, :] = two_parts(other + flip * mine)
        odd_ref[rows, :] = two_parts(mine - flip * other)
        return carry

    lax.fori_loop(0, mine_ref.shape[0] // MIX_ROWS, step, 0)


def split_groups(groups):
    outer = 1 << (groups.bit_length() - 1) // 2
    return outer, groups // outer


def transform(values, signs, samples):
    cols, rows = values.shape
    groups = rows // LOW
    outer, inner = split_groups(groups)
    hbm = pl.BlockSpec(memory_space=pltpu.HBM)
    return pl.pallas_call(
        functools.partial(transform_kernel, outer, inner),
        out_shape=[
            jax.ShapeDtypeStruct((groups * cols, LOW), jnp.float32),
            jax.ShapeDtypeStruct(samples.shape, samples.dtype),
        ],
        in_specs=[hbm, hbm, vmem()],
        out_specs=[vmem()] * 2,
        scratch_shapes=[
            pltpu.VMEM(values.shape, jnp.float32),
            pltpu.VMEM((rows // LANES, LANES), jnp.int32),
            pltpu.VMEM((groups * cols, LOW), jnp.float32),
            pltpu.VMEM((groups * cols, 2 * LOW), jnp.bfloat16),
            pltpu.SemaphoreType.DMA((outer + 1,)),
        ],
        compiler_params=pltpu.CompilerParams(vmem_limit_bytes=VMEM_LIMIT),
        cost_estimate=pl.CostEstimate(flops=4 * cols * rows * LOW, bytes_accessed=10 * cols * rows, transcendentals=0),
        name="transform",
    )(
        pltpu.with_memory_space_constraint(values, pltpu.HBM),
        pltpu.with_memory_space_constraint(signs.reshape(rows // LANES, LANES), pltpu.HBM),
        samples,
    )


def gather_cost(groups, cols, count, samp):
    return pl.CostEstimate(
        flops=4 * groups * cols * LOW * count * samp, bytes_accessed=4 * groups * cols * LOW, transcendentals=0
    )


def mix(mine, other):
    rows, low = mine.shape
    return pl.pallas_call(
        mix_kernel,
        out_shape=[jax.ShapeDtypeStruct((rows, 2 * low), jnp.bfloat16)] * 2,
        in_specs=[vmem()] * 2,
        out_specs=[vmem()] * 2,
        compiler_params=pltpu.CompilerParams(vmem_limit_bytes=VMEM_LIMIT),
        cost_estimate=pl.CostEstimate(flops=8 * rows * low, bytes_accessed=16 * rows * low, transcendentals=0),
        name="mix",
    )(mine, other)


def pick(first, groups, cols, tables, offsets, out_ref, at_row):
    count, samp = offsets.shape
    outer, inner = split_groups(groups)
    by_parity = [[t for t in range(count) if parity(first + t) == p] for p in range(2)]
    for table_ref, targets in zip(tables, by_parity):
        for at in range(0, len(targets), 2):
            pair = targets[at : at + 2]
            offset = jnp.concatenate([offsets[t : t + 1] for t in pair], axis=1)
            width = offset.shape[1]
            low = offset & (LOW - 1)
            high = jnp.broadcast_to(offset // LOW & (groups - 1), (cols, width))
            rows = lax.broadcasted_iota(jnp.int32, (LOW, width), 0)
            chosen = (rows == low).astype(jnp.float32).astype(jnp.bfloat16)
            chosen = jnp.concatenate([chosen, chosen], axis=0)
            picked = jnp.dot(table_ref[...], chosen, preferred_element_type=jnp.float32)
            sums = [jnp.zeros((cols, width), jnp.float32) for _ in range(2)]
            for g in range(groups):
                block = picked[g * cols : (g + 1) * cols]
                sums[g % 2] = jnp.where(high == g % outer * inner + g // outer, block, sums[g % 2])
            total = sums[0] + sums[1]
            for i, t in enumerate(pair):
                out_ref[at_row + t] = total[:, i * samp : (i + 1) * samp]


def place(values_ref, first, start, bits, first_piece, scale, out_ref):
    me = lax.axis_index("wide")
    for t in range(values_ref.shape[0] if start is None else start[1]):
        at = t if start is None else start[0] + t
        target = me ^ ladder_place(first + t, bits)
        common = target & me
        odd = common & 1
        for bit in range(1, bits):
            odd = odd ^ (common >> bit & 1)
        sign = (1 - 2 * odd).astype(jnp.float32) * scale
        out_ref[target - first_piece & (1 << bits) - 1] = values_ref[at] * sign


def early_kernel(firsts, groups, bits, first_piece, scale, even_ref, odd_ref, *refs):
    *offset_refs, out_ref, picked_ref = refs
    at_row = 0
    for first, offsets_ref in zip(firsts, offset_refs):
        count = offsets_ref.shape[0]
        pick(first, groups, out_ref.shape[1], (even_ref, odd_ref), offsets_ref[...], picked_ref, at_row)
        place(picked_ref, first, (at_row, count), bits, first_piece, scale, out_ref)
        at_row += count


def late_kernel(first, groups, bits, first_piece, scale, even_ref, odd_ref, offsets_ref, known_ref, out_ref, picked_ref):
    pick(first, groups, out_ref.shape[1], (even_ref, odd_ref), offsets_ref[...], picked_ref, 0)
    place(picked_ref, first, None, bits, first_piece, scale, out_ref)


def gather(firsts, groups, bits, first_piece, scale, even, odd, lists, known=None):
    count, samp = sum(offsets.shape[0] for offsets in lists), lists[0].shape[1]
    cols = even.shape[0] // groups
    if known is None:
        kernel, extra, aliases = functools.partial(early_kernel, firsts), (), {}
    else:
        kernel, extra, aliases = functools.partial(late_kernel, *firsts), (known,), {3: 0}
    return pl.pallas_call(
        functools.partial(kernel, groups, bits, first_piece, scale),
        out_shape=jax.ShapeDtypeStruct((1 << bits, cols, samp), jnp.float32),
        in_specs=[vmem()] * (2 + len(lists) + len(extra)),
        out_specs=vmem(),
        scratch_shapes=[pltpu.VMEM((count, cols, samp), jnp.float32)],
        input_output_aliases=aliases,
        compiler_params=pltpu.CompilerParams(vmem_limit_bytes=VMEM_LIMIT),
        cost_estimate=gather_cost(groups, cols, count, samp),
        name="gather",
    )(even, odd, *lists, *extra)


def per_device(panel, signs, samples):
    cols, rows = panel.shape
    samp = samples.shape[0]
    n_wide = lax.axis_size("wide")
    n_narrow = lax.axis_size("narrow")
    wide_bits = n_wide.bit_length() - 1
    narrow_bits = n_narrow.bit_length() - 1
    n_all = n_wide * n_narrow
    narrow_me = lax.axis_index("narrow")

    def across(values, mask):
        return lax.ppermute(values, AXES, [(i, i ^ mask) for i in range(n_all)])

    for bit in range(1, narrow_bits):
        if bit == 1:
            panel = panel * signs.astype(jnp.float32)[None, :]
            signs = jnp.ones_like(signs)
        upper = narrow_me >> bit & 1 == 1
        partner = across(panel, 1 << bit)
        panel = jnp.where(upper, partner - panel, panel + partner)

    groups = rows // LOW
    half, quarter = n_wide // 2, n_wide // 4
    ladder = list(reversed(range(wide_bits)))
    last = wide_bits - 1
    scale = 1.0 / math.sqrt(samp * n_all)
    first_piece = n_wide * 11 // 16
    plan = (groups, wide_bits, first_piece, scale)

    def exchange(values, i):
        return across(values, n_narrow << ladder[i] | 1)

    arrived = exchange(samples, 0)
    mine, listed = transform(panel, signs, samples)
    arrived, mine, listed = lax.optimization_barrier((arrived, mine, listed))
    other = across(mine, 1)
    asked = jnp.concatenate([listed, arrived])
    for i in range(1, last - 1):
        arrived = exchange(asked, i)
        if i == last - 2:
            even, odd = mix(mine, other)
            asked, arrived, even, odd = lax.optimization_barrier((asked, arrived, even, odd))
        asked = jnp.concatenate([asked, arrived])
    arrived = exchange(asked, last - 1)
    ahead = exchange(asked, last)
    late = exchange(arrived, last)
    lists = [asked.reshape(quarter, samp), arrived.reshape(quarter, samp), ahead.reshape(quarter, samp)]
    early = gather((0, quarter, half), *plan, even, odd, lists)
    late, early = lax.optimization_barrier((late, early))
    late = late.reshape(quarter, samp)

    pieces = gather((half + quarter,), *plan, even, odd, [late], early)
    order = [(p + first_piece) % n_wide for p in range(n_wide)]
    teams = [[w * n_narrow + (n ^ parity(w)) for w in order] for n in range(n_narrow)]
    pieces = lax.all_to_all(pieces, AXES, 0, 0, axis_index_groups=teams, tiled=True)
    return jnp.sum(pieces, axis=0)


def solution(mesh):
    in_specs = (P(None, AXES), P(AXES), P(AXES))
    return jax.shard_map(per_device, mesh=mesh, in_specs=in_specs, out_specs=P(None, AXES), check_vma=False)
```

```python
import functools
import math

import jax
import jax.numpy as jnp
from jax import lax
from jax.experimental import pallas as pl
from jax.experimental.pallas import tpu as pltpu
from jax.sharding import PartitionSpec as P

LANES = 128
LOW = 256
MIX_ROWS = 64
AXES = ("wide", "narrow")
VMEM_LIMIT = 40 << 20


def vmem():
    return pl.BlockSpec(memory_space=pltpu.VMEM)


def parity(value):
    return bin(value).count("1") & 1


def ladder_place(place, bits):
    return sum((place >> i & 1) << (bits - 1 - i) for i in range(bits))


def hadamard_rows(order):
    row = lax.broadcasted_iota(jnp.int32, (order, order), 0)
    col = lax.broadcasted_iota(jnp.int32, (order, order), 1)
    bits = row & col
    shift = order.bit_length() // 2
    while shift:
        bits = bits ^ (bits >> shift)
        shift //= 2
    sign = (1 - 2 * (bits & 1)).astype(jnp.float32).astype(jnp.bfloat16)
    return jnp.concatenate([sign, sign], axis=0)


def two_parts(values):
    high = values.astype(jnp.bfloat16)
    low = (values - high.astype(jnp.float32)).astype(jnp.bfloat16)
    return jnp.concatenate([high, low], axis=1)


def butterfly(values):
    values = list(values)
    step = 1
    while step < len(values):
        for at in range(len(values)):
            if not at & step:
                first, second = values[at], values[at | step]
                values[at], values[at | step] = first + second, first - second
        step *= 2
    return values


def first_pass(outer, inner, values_ref, signs_ref, mid, a):
    cols = values_ref.shape[0]
    tiles = LOW // LANES
    for tile in range(tiles):
        values = []
        for b in range(inner):
            at = (a * inner + b) * tiles + tile
            lanes = pl.ds(pl.multiple_of(at * LANES, LANES), LANES)
            values.append(values_ref[:, lanes] * signs_ref[pl.ds(at, 1), :].astype(jnp.float32))
        for b, value in enumerate(butterfly(values)):
            rows = pl.ds(pl.multiple_of((a * inner + b) * cols, cols), cols)
            mid[rows, tile * LANES : (tile + 1) * LANES] = value


def second_pass(outer, inner, cols, mid, parts):
    def step(b, carry):
        values = [mid[pl.ds(pl.multiple_of((a * inner + b) * cols, cols), cols), :] for a in range(outer)]
        block = two_parts(jnp.concatenate(butterfly(values), axis=0))
        parts[pl.ds(pl.multiple_of(b * outer * cols, outer * cols), outer * cols), :] = block
        return carry

    lax.fori_loop(0, inner, step, 0)


def transform_kernel(outer, inner, values_hbm, signs_hbm, samples_ref, out_ref, list_ref, values_ref, signs_ref, mid, parts, sems):
    cols, rows = values_hbm.shape
    block = rows // outer
    signs_copy = pltpu.make_async_copy(signs_hbm, signs_ref, sems.at[outer])
    copies = [
        pltpu.make_async_copy(
            values_hbm.at[:, pl.ds(a * block, block)], values_ref.at[:, pl.ds(a * block, block)], sems.at[a]
        )
        for a in range(outer)
    ]
    signs_copy.start()
    for copy in copies:
        copy.start()
    list_ref[...] = samples_ref[...]
    matrix = hadamard_rows(LOW)
    signs_copy.wait()
    for a, copy in enumerate(copies):
        copy.wait()
        first_pass(outer, inner, values_ref, signs_ref, mid, a)
    second_pass(outer, inner, cols, mid, parts)
    out_ref[...] = jnp.dot(parts[...], matrix, preferred_element_type=jnp.float32)


def mix_kernel(mine_ref, other_ref, even_ref, odd_ref):
    core = lax.axis_index("narrow") & 1
    flip = (1 - 2 * core).astype(jnp.float32)

    def step(at, carry):
        rows = pl.ds(pl.multiple_of(at * MIX_ROWS, MIX_ROWS), MIX_ROWS)
        mine, other = mine_ref[rows, :], other_ref[rows, :]
        even_ref[rows, :] = two_parts(other + flip * mine)
        odd_ref[rows, :] = two_parts(mine - flip * other)
        return carry

    lax.fori_loop(0, mine_ref.shape[0] // MIX_ROWS, step, 0)


def split_groups(groups):
    outer = 1 << (groups.bit_length() - 1) // 2
    return outer, groups // outer


def transform(values, signs, samples):
    cols, rows = values.shape
    groups = rows // LOW
    outer, inner = split_groups(groups)
    hbm = pl.BlockSpec(memory_space=pltpu.HBM)
    return pl.pallas_call(
        functools.partial(transform_kernel, outer, inner),
        out_shape=[
            jax.ShapeDtypeStruct((groups * cols, LOW), jnp.float32),
            jax.ShapeDtypeStruct(samples.shape, samples.dtype),
        ],
        in_specs=[hbm, hbm, vmem()],
        out_specs=[vmem()] * 2,
        scratch_shapes=[
            pltpu.VMEM(values.shape, jnp.float32),
            pltpu.VMEM((rows // LANES, LANES), jnp.int32),
            pltpu.VMEM((groups * cols, LOW), jnp.float32),
            pltpu.VMEM((groups * cols, 2 * LOW), jnp.bfloat16),
            pltpu.SemaphoreType.DMA((outer + 1,)),
        ],
        compiler_params=pltpu.CompilerParams(vmem_limit_bytes=VMEM_LIMIT),
        cost_estimate=pl.CostEstimate(flops=4 * cols * rows * LOW, bytes_accessed=10 * cols * rows, transcendentals=0),
        name="transform",
    )(
        pltpu.with_memory_space_constraint(values, pltpu.HBM),
        pltpu.with_memory_space_constraint(signs.reshape(rows // LANES, LANES), pltpu.HBM),
        samples,
    )


def gather_cost(groups, cols, count, samp):
    return pl.CostEstimate(
        flops=4 * groups * cols * LOW * count * samp, bytes_accessed=4 * groups * cols * LOW, transcendentals=0
    )


def mix(mine, other):
    rows, low = mine.shape
    return pl.pallas_call(
        mix_kernel,
        out_shape=[jax.ShapeDtypeStruct((rows, 2 * low), jnp.bfloat16)] * 2,
        in_specs=[vmem()] * 2,
        out_specs=[vmem()] * 2,
        compiler_params=pltpu.CompilerParams(vmem_limit_bytes=VMEM_LIMIT),
        cost_estimate=pl.CostEstimate(flops=8 * rows * low, bytes_accessed=16 * rows * low, transcendentals=0),
        name="mix",
    )(mine, other)


def pick(first, groups, cols, tables, offsets, out_ref, at_row):
    count, samp = offsets.shape
    outer, inner = split_groups(groups)
    by_parity = [[t for t in range(count) if parity(first + t) == p] for p in range(2)]
    for table_ref, targets in zip(tables, by_parity):
        for at in range(0, len(targets), 2):
            pair = targets[at : at + 2]
            offset = jnp.concatenate([offsets[t : t + 1] for t in pair], axis=1)
            width = offset.shape[1]
            low = offset & (LOW - 1)
            high = jnp.broadcast_to(offset // LOW & (groups - 1), (cols, width))
            rows = lax.broadcasted_iota(jnp.int32, (LOW, width), 0)
            chosen = (rows == low).astype(jnp.float32).astype(jnp.bfloat16)
            chosen = jnp.concatenate([chosen, chosen], axis=0)
            picked = jnp.dot(table_ref[...], chosen, preferred_element_type=jnp.float32)
            sums = [jnp.zeros((cols, width), jnp.float32) for _ in range(2)]
            for g in range(groups):
                block = picked[g * cols : (g + 1) * cols]
                sums[g % 2] = jnp.where(high == g % outer * inner + g // outer, block, sums[g % 2])
            total = sums[0] + sums[1]
            for i, t in enumerate(pair):
                out_ref[at_row + t] = total[:, i * samp : (i + 1) * samp]


def early_kernel(firsts, groups, even_ref, odd_ref, *refs):
    *offset_refs, out_ref = refs
    at_row = 0
    for first, offsets_ref in zip(firsts, offset_refs):
        pick(first, groups, out_ref.shape[1], (even_ref, odd_ref), offsets_ref[...], out_ref, at_row)
        at_row += offsets_ref.shape[0]


def gather_kernel(first, groups, bits, first_piece, scale, even_ref, odd_ref, offsets_ref, *refs):
    *known_refs, out_ref, late_ref = refs
    cols = out_ref.shape[1]
    me = lax.axis_index("wide")

    team = lax.axis_index("narrow") & 1
    for bit in range(bits):
        team = team ^ (me >> bit & 1)
    first_of_team = jnp.where(team == 0, first_piece, (1 << bits) - 1)

    def place(place_of, value):
        target = me ^ place_of
        common = target & me
        odd = common & 1
        for bit in range(1, bits):
            odd = odd ^ (common >> bit & 1)
        out_ref[target - first_of_team & (1 << bits) - 1] = value * ((1 - 2 * odd).astype(jnp.float32) * scale)

    pick(first, groups, cols, (even_ref, odd_ref), offsets_ref[...], late_ref, 0)
    at_place = 0
    for ref in (*known_refs, late_ref):
        for t in range(ref.shape[0]):
            place(ladder_place(at_place, bits), ref[t])
            at_place += 1


def gather_early(firsts, groups, even, odd, lists):
    count, samp = sum(offsets.shape[0] for offsets in lists), lists[0].shape[1]
    cols = even.shape[0] // groups
    return pl.pallas_call(
        functools.partial(early_kernel, firsts, groups),
        out_shape=jax.ShapeDtypeStruct((count, cols, samp), jnp.float32),
        in_specs=[vmem()] * (2 + len(lists)),
        out_specs=vmem(),
        compiler_params=pltpu.CompilerParams(vmem_limit_bytes=VMEM_LIMIT),
        cost_estimate=gather_cost(groups, cols, count, samp),
        name="gather_early",
    )(even, odd, *lists)


def gather(first, groups, bits, first_piece, scale, even, odd, offsets, known):
    count, samp = offsets.shape
    cols = even.shape[0] // groups
    return pl.pallas_call(
        functools.partial(gather_kernel, first, groups, bits, first_piece, scale),
        out_shape=jax.ShapeDtypeStruct((first + count, cols, samp), jnp.float32),
        in_specs=[vmem()] * (3 + len(known)),
        out_specs=vmem(),
        scratch_shapes=[pltpu.VMEM((count, cols, samp), jnp.float32)],
        compiler_params=pltpu.CompilerParams(vmem_limit_bytes=VMEM_LIMIT),
        cost_estimate=gather_cost(groups, cols, count, samp),
        name="gather",
    )(even, odd, offsets, *known)


def per_device(panel, signs, samples):
    cols, rows = panel.shape
    samp = samples.shape[0]
    n_wide = lax.axis_size("wide")
    n_narrow = lax.axis_size("narrow")
    wide_bits = n_wide.bit_length() - 1
    narrow_bits = n_narrow.bit_length() - 1
    n_all = n_wide * n_narrow
    narrow_me = lax.axis_index("narrow")

    def across(values, mask):
        return lax.ppermute(values, AXES, [(i, i ^ mask) for i in range(n_all)])

    for bit in range(1, narrow_bits):
        if bit == 1:
            panel = panel * signs.astype(jnp.float32)[None, :]
            signs = jnp.ones_like(signs)
        upper = narrow_me >> bit & 1 == 1
        partner = across(panel, 1 << bit)
        panel = jnp.where(upper, partner - panel, panel + partner)

    groups = rows // LOW
    half, quarter = n_wide // 2, n_wide // 4
    ladder = list(reversed(range(wide_bits)))
    last = wide_bits - 1

    def exchange(values, i):
        return across(values, n_narrow << ladder[i] | 1)

    arrived = exchange(samples, 0)
    mine, listed = transform(panel, signs, samples)
    arrived, mine, listed = lax.optimization_barrier((arrived, mine, listed))
    other = across(mine, 1)
    asked = jnp.concatenate([listed, arrived])
    for i in range(1, last - 1):
        arrived = exchange(asked, i)
        if i == last - 2:
            even, odd = mix(mine, other)
            asked, arrived, even, odd = lax.optimization_barrier((asked, arrived, even, odd))
        asked = jnp.concatenate([asked, arrived])
    arrived = exchange(asked, last - 1)
    ahead = exchange(asked, last)
    late = exchange(arrived, last)
    lists = [asked.reshape(quarter, samp), arrived.reshape(quarter, samp), ahead.reshape(quarter, samp)]
    early = [gather_early((0, quarter, half), groups, even, odd, lists)]
    late, *early = lax.optimization_barrier((late, *early))
    late = late.reshape(quarter, samp)

    scale = 1.0 / math.sqrt(samp * n_all)
    first_piece = n_wide * 11 // 16
    pieces = gather(half + quarter, groups, wide_bits, first_piece, scale, even, odd, late, early)
    firsts = (first_piece, n_wide - 1)
    teams = [
        [w * n_narrow + (n ^ parity(w)) for w in ((p + firsts[n & 1]) % n_wide for p in range(n_wide))]
        for n in range(n_narrow)
    ]
    pieces = lax.all_to_all(pieces, AXES, 0, 0, axis_index_groups=teams, tiled=True)
    return jnp.sum(pieces, axis=0)


def solution(mesh):
    in_specs = (P(None, AXES), P(AXES), P(AXES))
    return jax.shard_map(per_device, mesh=mesh, in_specs=in_specs, out_specs=P(None, AXES), check_vma=False)
```
